32 devices in a mesh: line: 2 (over y), gather: 16 (over z, x, core).
Axes of the slice: x: 2, y: 2, z: 4, core: 2. Of those that a mesh axis runs over, the one named last changes fastest.
Arguments:
- noisy: bfloat16 [2, 16, 256, 256], P('line', 'gather'), may hold values from -6 to 6
- target: float32 [2, 16, 256, 256], P('line', None, 'gather'), may hold values from -6 to 6
- in_weight: bfloat16 [64, 4], replicated, may hold values from -3 to 3
- in_bias: float32 [64], replicated, may hold values from -3 to 3
- mid_weight: bfloat16 [3, 3, 64, 64], replicated, may hold values from -0.25 to 0.25
- mid_bias: float32 [64], replicated, may hold values from -3 to 3
- dec_weight: bfloat16 [3, 3, 64, 64], replicated, may hold values from -0.25 to 0.25
- dec_bias: float32 [64], replicated, may hold values from -3 to 3
- out_weight: bfloat16 [4, 64], replicated, may hold values from -0.75 to 0.75
- out_bias: float32 [4], replicated, may hold values from -3 to 3
Outputs:
- residual_map: float32 [2, 16, 256, 256], P('line', None, 'gather')
- in_weight_grad: float32 [64, 4], replicated
- in_bias_grad: float32 [64], replicated
- mid_weight_grad: float32 [3, 3, 64, 64], replicated
- mid_bias_grad: float32 [64], replicated
- dec_weight_grad: float32 [3, 3, 64, 64], replicated
- dec_bias_grad: float32 [64], replicated
- out_weight_grad: float32 [4, 64], replicated
- out_bias_grad: float32 [4], replicated
The draws below stay inside these ranges and needn't reach their ends.
All inputs are finite; a program needn't handle non-finite values.
Results may differ from the reference program's by a relative error of at most 0.0014.
Values may be sent and summed in bfloat16 or wider, within the bound.
A program may use at most 128 MiB of HBM per device.

```python
import math
import jax
import jax.numpy as jnp
from jax import lax

C = 64
R = 256
NT = 256
SHOTS = 16
LINES = 2
N_LINE = 2
N_GATHER = 16


def block_scale(own_key, shape, pieces, least, top_value):
    def one(dim, parts):
        steps = jax.random.uniform(jax.random.fold_in(jax.random.fold_in(own_key, 6), dim), (parts,), jnp.float32, least / len(pieces), top_value / len(pieces))
        return jnp.repeat(jnp.exp(steps), shape[dim] // parts).reshape((-1,) + (1,) * (len(shape) - dim - 1))

    gain = one(*pieces[0])
    for cut in pieces[1:]:
        gain = gain * one(*cut)
    return gain


def scatter_about(own_key, shape, scale, most, pieces=(), kind=jnp.bfloat16):
    result = jax.random.normal(own_key, shape, jnp.float32) * scale
    if len(pieces) > 0:
        result = block_scale(own_key, shape, pieces, -0.22, 0.18) * result
    return jnp.clip(result, min=-most, max=most).astype(kind)


def setup_inputs(seed: int = 0) -> dict:
    keys = jax.random.split(jax.random.key(seed), 11)
    noisy = scatter_about(keys[0], (LINES, SHOTS, R, NT), 1.0, 6.0, ((0, 2), (1, 16)))
    target = scatter_about(keys[1], (LINES, SHOTS, R, NT), 1.0, 6.0, ((0, 2), (2, 16)), jnp.float32)
    in_weight = scatter_about(keys[2], (C, 4), 4 ** -0.5, 3.0)
    in_bias = scatter_about(keys[3], (C,), 0.5, 3.0, (), jnp.float32)
    mid_weight = scatter_about(keys[4], (3, 3, C, C), (9 * C) ** -0.5, 0.25)
    mid_bias = scatter_about(keys[5], (C,), 0.5, 3.0, (), jnp.float32)
    dec_weight = scatter_about(keys[6], (3, 3, C, C), (9 * C) ** -0.5, 0.25)
    dec_bias = scatter_about(keys[7], (C,), 0.5, 3.0, (), jnp.float32)
    out_weight = scatter_about(keys[8], (4, C), C ** -0.5, 0.75)
    out_bias = scatter_about(keys[9], (4,), 0.5, 3.0, (), jnp.float32)
    return dict(noisy=noisy, target=target, in_weight=in_weight, in_bias=in_bias, mid_weight=mid_weight, mid_bias=mid_bias, dec_weight=dec_weight, dec_bias=dec_bias, out_weight=out_weight, out_bias=out_bias)


def conv_valid(inputs, weights, axis):
    count_rows = inputs.shape[axis] - 2
    steps_time = inputs.shape[3]
    padded = jnp.pad(inputs.astype(jnp.float32), ((0, 0), (0, 0), (0, 0), (1, 1)))
    wide_weights = weights.astype(jnp.float32)
    summed = None
    for row_tap in range(3):
        band_rows = lax.slice_in_dim(padded, row_tap, row_tap + count_rows, axis=axis)
        for col_tap in range(3):
            term = jnp.einsum('dc,xyct->xydt', wide_weights[row_tap, col_tap], band_rows[..., col_tap:col_tap + steps_time])
            summed = term if summed is None else summed + term
    return summed

def first_layer(samples, in_weight, in_bias):
    shots_here, recv_here, time_here = samples.shape
    cells = samples.reshape(shots_here, recv_here // 2, 2, time_here // 2, 2)
    cells = cells.transpose(0, 1, 2, 4, 3).reshape(shots_here, recv_here // 2, 4, time_here // 2)
    pre_one = jnp.einsum('dk,arkt->ardt', in_weight.astype(jnp.float32), cells.astype(jnp.float32))
    pre_one = pre_one + in_bias[:, None]
    return jax.nn.silu(pre_one).astype(jnp.bfloat16)

def second_layer(rimmed, mid_weight, mid_bias):
    pre_two = conv_valid(rimmed, mid_weight, 1) + mid_bias[:, None]
    return jax.nn.silu(pre_two).astype(jnp.bfloat16)

def encoder(samples, in_weight, in_bias, mid_weight, mid_bias):
    hidden = first_layer(samples, in_weight, in_bias)
    rimmed = jnp.pad(hidden, ((0, 0), (1, 1), (0, 0), (0, 0)))
    return second_layer(rimmed, mid_weight, mid_bias)

def decoder(latent, dec_weight, dec_bias, out_weight, out_bias):
    padded = jnp.pad(latent, ((1, 1), (0, 0), (0, 0), (0, 0)))
    pre_three = conv_valid(padded, dec_weight, 0) + dec_bias[:, None]
    upper = jax.nn.silu(pre_three).astype(jnp.bfloat16)
    cells = jnp.einsum('kd,srdt->srkt', out_weight.astype(jnp.float32), upper.astype(jnp.float32))
    cells = cells + out_bias[:, None]
    shots_here, recv_here, four_taps, time_here = cells.shape
    cells = cells.reshape(shots_here, recv_here, 2, 2, time_here).transpose(0, 1, 2, 4, 3)
    return cells.reshape(shots_here, 2 * recv_here, 2 * time_here)

def reference(noisy, target, in_weight, in_bias, mid_weight, mid_bias, dec_weight, dec_bias, out_weight, out_bias):
    loss_scale = 1.0 / math.sqrt(N_LINE * N_GATHER * R * NT)
    enc_params = tuple((p.astype(jnp.float32) for p in (in_weight, in_bias, mid_weight, mid_bias)))
    dec_params = tuple((p.astype(jnp.float32) for p in (dec_weight, dec_bias, out_weight, out_bias)))
    half_recv = R // 2
    half_time = NT // 2
    blocks = half_recv // 2
    residual_lines = []
    enc_total = None
    dec_total = None
    for line in range(N_LINE):
        shots = noisy[line]
        latent = lax.map(lambda single: encoder(single[None], *enc_params)[0], shots)
        lat_blocks = latent.reshape(N_GATHER, blocks, 2, C, half_time).transpose(1, 0, 2, 3, 4)
        tgt_blocks = target[line].reshape(N_GATHER, blocks, 4, NT).transpose(1, 0, 2, 3)

        def dec_step(block_item):
            latent_block, truth_block = block_item
            predicted, dec_pull = jax.vjp(decoder, latent_block, *dec_params)
            residual = predicted - truth_block
            return (residual, dec_pull(residual * loss_scale))
        residual_blocks, dec_cots = lax.map(dec_step, (lat_blocks, tgt_blocks))
        residual_lines.append(residual_blocks.transpose(1, 0, 2, 3).reshape(N_GATHER, R, NT))
        latent_cots = dec_cots[0].transpose(1, 0, 2, 3, 4).reshape(N_GATHER, half_recv, C, half_time)
        dec_grads = tuple((lax.optimization_barrier(jnp.sum(g, axis=0)) for g in dec_cots[1:]))

        def enc_step(shot_item):
            single, cotangent = shot_item
            unused, enc_pull = jax.vjp(lambda *params: encoder(single[None], *params), *enc_params)
            return enc_pull(cotangent[None])
        enc_grads = tuple((lax.optimization_barrier(jnp.sum(g, axis=0)) for g in lax.map(enc_step, (shots, latent_cots))))
        if enc_total is None:
            enc_total, dec_total = (enc_grads, dec_grads)
        else:
            enc_total = tuple((a + b for a, b in zip(enc_total, enc_grads)))
            dec_total = tuple((a + b for a, b in zip(dec_total, dec_grads)))
    residual_map = jnp.stack(residual_lines)
    return (residual_map, enc_total[0], enc_total[1], enc_total[2], enc_total[3], dec_total[0], dec_total[1], dec_total[2], dec_total[3])
```

```python
import functools
import math

import jax
import jax.numpy as jnp
from jax import lax
from jax.experimental import pallas as pl
from jax.experimental.pallas import tpu as pltpu
from jax.sharding import PartitionSpec as P

MESH = pl.DeviceIdType.MESH
BF = jnp.bfloat16
F32 = jnp.float32


def exchange_kernel(n, x_ref, out_ref, held, send_sem, recv_sem):
    line = lax.axis_index("line")
    me = lax.axis_index("gather")
    barrier = pltpu.get_barrier_semaphore()

    def greet(k, carry):
        peer = lax.rem(me + k, n)
        pl.semaphore_signal(barrier, inc=1, device_id=(line, peer), device_id_type=MESH)
        return carry

    lax.fori_loop(1, n, greet, 0)
    pl.semaphore_wait(barrier, n - 1)

    def copy(src, slot, peer, sem):
        return pltpu.make_async_remote_copy(
            src_ref=x_ref.at[src],
            dst_ref=held.at[slot],
            send_sem=send_sem.at[sem],
            recv_sem=recv_sem.at[slot],
            device_id=(line, peer),
            device_id_type=MESH,
        )

    def send(k, carry):
        peer = lax.rem(me + k, n)
        copy(peer, me, peer, k).start()
        return carry

    lax.fori_loop(1, n, send, 0)
    out_ref[pl.ds(me, 1)] = x_ref[pl.ds(me, 1)]

    def finish(k, carry):
        peer = lax.rem(me + k, n)
        source = lax.rem(me + n - k, n)
        copy(peer, source, peer, k).wait_recv()
        copy(peer, source, peer, k).wait_send()
        out_ref[pl.ds(source, 1)] = held[pl.ds(source, 1)]
        return carry

    lax.fori_loop(1, n, finish, 0)


def exchange(x):
    n = x.shape[0]
    return pl.pallas_call(
        functools.partial(exchange_kernel, n),
        out_shape=jax.ShapeDtypeStruct(x.shape, x.dtype),
        in_specs=[pl.BlockSpec(memory_space=pltpu.VMEM)],
        out_specs=pl.BlockSpec(memory_space=pltpu.VMEM),
        scratch_shapes=[
            pltpu.VMEM(x.shape, x.dtype),
            pltpu.SemaphoreType.DMA((n,)),
            pltpu.SemaphoreType.DMA((n,)),
        ],
        compiler_params=pltpu.CompilerParams(
            collective_id=0, has_side_effects=True, vmem_limit_bytes=16 << 20
        ),
    )(x)


def total_kernel(nd, n, x_ref, out_ref, held, result, send_sem, recv_sem, back_sem, done_sem):
    me = lax.axis_index("line") * n + lax.axis_index("gather")

    def at(peer):
        return (peer // n, lax.rem(peer, n))

    barrier = pltpu.get_barrier_semaphore()

    def greet(k, carry):
        peer = lax.rem(me + k, nd)
        pl.semaphore_signal(barrier, inc=1, device_id=at(peer), device_id_type=MESH)
        return carry

    lax.fori_loop(1, nd, greet, 0)
    pl.semaphore_wait(barrier, nd - 1)

    def part(src, slot, peer, sem):
        return pltpu.make_async_remote_copy(
            src_ref=x_ref.at[src],
            dst_ref=held.at[slot],
            send_sem=send_sem.at[sem],
            recv_sem=recv_sem.at[slot],
            device_id=at(peer),
            device_id_type=MESH,
        )

    def whole(slot, peer, sem):
        return pltpu.make_async_remote_copy(
            src_ref=result.at[slot],
            dst_ref=result.at[slot],
            send_sem=back_sem.at[sem],
            recv_sem=done_sem.at[slot],
            device_id=at(peer),
            device_id_type=MESH,
        )

    def send(k, carry):
        peer = lax.rem(me + k, nd)
        part(peer, me, peer, k).start()
        return carry

    lax.fori_loop(1, nd, send, 0)

    def add(k, acc):
        source = lax.rem(me + nd - k, nd)
        part(source, source, source, k).wait_recv()
        return acc + held[pl.ds(source, 1)]

    result[pl.ds(me, 1)] = lax.fori_loop(1, nd, add, x_ref[pl.ds(me, 1)])

    def spread(k, carry):
        peer = lax.rem(me + k, nd)
        whole(me, peer, k).start()
        return carry

    lax.fori_loop(1, nd, spread, 0)

    def finish(k, carry):
        peer = lax.rem(me + k, nd)
        source = lax.rem(me + nd - k, nd)
        part(peer, me, peer, k).wait_send()
        whole(me, peer, k).wait_send()
        whole(source, peer, k).wait_recv()
        return carry

    lax.fori_loop(1, nd, finish, 0)
    out_ref[...] = result[...]


def total(x, n):
    nd = x.shape[0]
    sems = pltpu.SemaphoreType.DMA((nd,))
    return pl.pallas_call(
        functools.partial(total_kernel, nd, n),
        out_shape=jax.ShapeDtypeStruct(x.shape, x.dtype),
        in_specs=[pl.BlockSpec(memory_space=pltpu.VMEM)],
        out_specs=pl.BlockSpec(memory_space=pltpu.VMEM),
        scratch_shapes=[
            pltpu.VMEM(x.shape, x.dtype),
            pltpu.VMEM(x.shape, x.dtype),
            sems,
            sems,
            sems,
            sems,
        ],
        compiler_params=pltpu.CompilerParams(
            collective_id=1, has_side_effects=True, vmem_limit_bytes=16 << 20
        ),
    )(x)


def gate(pre):
    sig = 1.0 / (1.0 + jnp.exp(-pre))
    act = pre * sig
    return act, sig + act * (1.0 - sig)


def dot(a, b):
    return jnp.dot(a, b, preferred_element_type=F32)


def dot_t(a, b):
    return lax.dot_general(a, b, (((1,), (1,)), ((), ())), preferred_element_type=F32)


def exact_dot(x, onehot):
    hi = x.astype(BF)
    rest = x - hi.astype(F32)
    mid = rest.astype(BF)
    low = (rest - mid.astype(F32)).astype(BF)
    return dot(hi, onehot) + dot(mid, onehot) + dot(low, onehot)


def step_kernel(
    scale,
    a_ref,
    target_ref,
    win_ref,
    w2_ref,
    w3_ref,
    v2_ref,
    v3_ref,
    wout_ref,
    woutt_ref,
    ib_ref,
    mb_ref,
    db_ref,
    ob_ref,
    edge_ref,
    deint_ref,
    inter_ref,
    res_ref,
    g2_ref,
    g3_ref,
    gin_ref,
    gout_ref,
    gob_ref,
    gmb_ref,
    gdb_ref,
    h_ref,
    z_ref,
    e3_ref,
    e2_ref,
    e1_ref,
    h3_ref,
    s1_ref,
    s2_ref,
    s3_ref,
):
    shots, rows = target_ref.shape[0], target_ref.shape[1]
    rl = rows // 2
    hr = rl + 2
    c = ib_ref.shape[0]
    t = ib_ref.shape[1]
    lane = lax.broadcasted_iota(jnp.int32, (c, t), 1)
    first, last = lane == 0, lane == t - 1

    def later(x):
        return jnp.where(first, 0.0, pltpu.roll(x, 1, 1)).astype(BF)

    def sooner(x):
        return jnp.where(last, 0.0, pltpu.roll(x, t - 1, 1)).astype(BF)

    def band(ref, r):
        return ref[r : r + 3].reshape(3 * 3 * c, t)

    for r in range(rl):
        for slot in (0, shots + 1):
            z_ref[r, slot] = jnp.zeros((3 * c, t), BF)
            e3_ref[r, slot] = jnp.zeros((3 * c, t), BF)
    for slot in (0, 1, rl + 2, rl + 3):
        e2_ref[slot] = jnp.zeros((3 * c, t), BF)
    for ref in (g2_ref, g3_ref, gin_ref, gout_ref, gob_ref, gmb_ref, gdb_ref):
        ref[...] = jnp.zeros_like(ref)

    def encode(s, carry):
        pre1 = dot(win_ref[...], a_ref[s])
        for r in range(hr):
            act, slope = gate(pre1[r * c : (r + 1) * c] + ib_ref[...])
            if r == 0:
                act, slope = act * edge_ref[0:1], slope * edge_ref[0:1]
            if r == hr - 1:
                act, slope = act * edge_ref[1:2], slope * edge_ref[1:2]
            s1_ref[s, r] = slope
            h_ref[s, r, 0:c] = later(act)
            h_ref[s, r, c : 2 * c] = act.astype(BF)
            h_ref[s, r, 2 * c : 3 * c] = sooner(act)
        for r in range(0, rl, 2):
            wide = jnp.concatenate(
                [h_ref[s, r + q : r + q + 3].reshape(9 * c, t) for q in range(2)], axis=1
            )
            pre2 = dot(w2_ref[...], wide)
            for q in range(2):
                act, slope = gate(pre2[:, q * t : (q + 1) * t] + mb_ref[...])
                s2_ref[s, r + q] = slope
                z_ref[r + q, s + 1, 0:c] = later(act)
                z_ref[r + q, s + 1, c : 2 * c] = act.astype(BF)
                z_ref[r + q, s + 1, 2 * c : 3 * c] = sooner(act)
        return carry

    lax.fori_loop(0, shots, encode, 0)

    def decode(s, carry):
        for r in range(0, rl, 2):
            wide = jnp.concatenate(
                [z_ref[r + q, pl.ds(s, 3)].reshape(9 * c, t) for q in range(2)], axis=1
            )
            pre3 = dot(w3_ref[...], wide)
            for q in range(2):
                act, slope = gate(pre3[:, q * t : (q + 1) * t] + db_ref[...])
                s3_ref[r + q] = slope
                h3_ref[(r + q) * c : (r + q + 1) * c] = act.astype(BF)
        truth = exact_dot(target_ref[s], deint_ref[...])
        truth = jnp.concatenate([truth[:, :t], truth[:, t:]], axis=0)
        resid = dot(wout_ref[...], h3_ref[...]) + ob_ref[...] - truth
        side = jnp.concatenate([resid[:rows], resid[rows:]], axis=1)
        res_ref[s] = exact_dot(side, inter_ref[...])
        g = resid * scale
        gob_ref[...] += g
        g = g.astype(BF)
        gout_ref[...] += dot_t(g, h3_ref[...])
        back3 = dot(woutt_ref[...], g)
        bias = gdb_ref[...]
        for r in range(rl):
            e = back3[r * c : (r + 1) * c].astype(BF).astype(F32) * s3_ref[r]
            bias = bias + e
            e3_ref[r, s + 1, 0:c] = sooner(e)
            e3_ref[r, s + 1, c : 2 * c] = e.astype(BF)
            e3_ref[r, s + 1, 2 * c : 3 * c] = later(e)
        gdb_ref[...] = bias
        left = jnp.concatenate([e3_ref[r, s + 1] for r in range(rl)], axis=1)
        right = jnp.concatenate(
            [z_ref[r, pl.ds(s, 3), c : 2 * c].reshape(3 * c, t) for r in range(rl)], axis=1
        )
        g3_ref[...] += dot_t(left, right)
        return carry

    lax.fori_loop(0, shots, decode, 0)

    def pull(s, carry):
        bias = gmb_ref[...]
        for r in range(0, rl, 2):
            wide = jnp.concatenate(
                [e3_ref[r + q, pl.ds(s, 3)].reshape(9 * c, t) for q in range(2)], axis=1
            )
            back2 = dot(v3_ref[...], wide)
            for q in range(2):
                e = back2[:, q * t : (q + 1) * t].astype(BF).astype(F32) * s2_ref[s, r + q]
                bias = bias + e
                e2_ref[r + q + 2, 0:c] = sooner(e)
                e2_ref[r + q + 2, c : 2 * c] = e.astype(BF)
                e2_ref[r + q + 2, 2 * c : 3 * c] = later(e)
        gmb_ref[...] = bias
        left = jnp.concatenate([e2_ref[r + 2] for r in range(rl)], axis=1)
        right = jnp.concatenate(
            [h_ref[s, r : r + 3, c : 2 * c].reshape(3 * c, t) for r in range(rl)], axis=1
        )
        g2_ref[...] += dot_t(left, right)
        for r in range(0, hr, 2):
            wide = jnp.concatenate(
                [e2_ref[r + q : r + q + 3].reshape(9 * c, t) for q in range(2)], axis=1
            )
            back1 = dot(v2_ref[...], wide)
            for q in range(2):
                e = back1[:, q * t : (q + 1) * t].astype(BF).astype(F32) * s1_ref[s, r + q]
                e1_ref[(r + q) * c : (r + q + 1) * c] = e.astype(BF)
        gin_ref[...] += dot_t(e1_ref[...], a_ref[s])
        return carry

    lax.fori_loop(0, shots, pull, 0)


def step(scale, operands, shots, rows, c, t, ka):
    rl = rows // 2
    hr = rl + 2
    vmem = pl.BlockSpec(memory_space=pltpu.VMEM)
    shape = jax.ShapeDtypeStruct
    outs = (
        shape((shots, rows, 2 * t), F32),
        shape((3 * c, 3 * c), F32),
        shape((3 * c, 3 * c), F32),
        shape((hr * c, ka), F32),
        shape((2 * rows, rl * c), F32),
        shape((2 * rows, t), F32),
        shape((c, t), F32),
        shape((c, t), F32),
    )
    flops = 2 * 6 * 9 * c * c * shots * rl * t
    return pl.pallas_call(
        functools.partial(step_kernel, scale),
        out_shape=outs,
        in_specs=[vmem] * len(operands),
        out_specs=(vmem,) * len(outs),
        scratch_shapes=[
            pltpu.VMEM((shots, hr, 3 * c, t), BF),
            pltpu.VMEM((rl, shots + 2, 3 * c, t), BF),
            pltpu.VMEM((rl, shots + 2, 3 * c, t), BF),
            pltpu.VMEM((rl + 4, 3 * c, t), BF),
            pltpu.VMEM((hr * c, t), BF),
            pltpu.VMEM((rl * c, t), BF),
            pltpu.VMEM((shots, hr, c, t), F32),
            pltpu.VMEM((shots, rl, c, t), F32),
            pltpu.VMEM((rl, c, t), F32),
        ],
        compiler_params=pltpu.CompilerParams(vmem_limit_bytes=56 << 20),
        cost_estimate=pl.CostEstimate(
            flops=flops, bytes_accessed=8 << 20, transcendentals=3 * c * shots * rl * t
        ),
    )(*operands)


def per_device(noisy, target, in_w, in_b, mid_w, mid_b, dec_w, dec_b, out_w, out_b):
    lines, n = lax.axis_size("line"), lax.axis_size("gather")
    nd = lines * n
    recv, nt = noisy.shape[2], noisy.shape[3]
    shots, rows = target.shape[1], target.shape[2]
    c, t, rl = in_w.shape[0], nt // 2, rows // 2
    hr = rl + 2
    scale = 1.0 / math.sqrt(lines * n * recv * nt)
    me = lax.axis_index("gather")
    ka = -(-(4 * hr + 1) // 16) * 16

    when = jnp.arange(nt)
    deint = (when[:, None] == (2 * (when % t) + when // t)[None, :]).astype(BF)
    inter = deint.T
    wanted = (jnp.arange(n)[:, None] * rows + jnp.arange(2 * hr)[None, :] - 2).reshape(-1)
    select = (wanted[:, None] == jnp.arange(recv)[None, :]).astype(BF)
    picked = dot(select, noisy[0, 0]).astype(BF)
    picked = dot(picked, deint).astype(BF).reshape(n, 2 * hr, nt)
    tail = jnp.zeros((n, ka - 4 * hr, t), BF).at[:, 0].set(1.0)
    blocks = jnp.concatenate([picked[..., :t], picked[..., t:], tail], axis=1)
    cells = exchange(blocks)

    iw = in_w.reshape(c, 2, 2)
    win = jnp.einsum("rq,dij->rdjqi", jnp.eye(hr, dtype=BF), iw).reshape(hr * c, 4 * hr)
    win = jnp.pad(win, ((0, 0), (0, ka - 4 * hr)))
    ow = out_w.reshape(2, 2, c)
    wout = jnp.einsum("rq,ijd->jqird", jnp.eye(rl, dtype=BF), ow).reshape(2 * rows, rl * c)
    ob = jnp.broadcast_to(out_b.reshape(2, 2).T[:, None, :], (2, rl, 2)).reshape(2 * rows, 1)
    w2 = mid_w.transpose(2, 0, 1, 3).reshape(c, 9 * c)
    w3 = dec_w.transpose(2, 0, 1, 3).reshape(c, 9 * c)
    v2 = mid_w[::-1].transpose(3, 0, 1, 2).reshape(c, 9 * c)
    v3 = dec_w[::-1].transpose(3, 0, 1, 2).reshape(c, 9 * c)
    edge = jnp.stack([me > 0, me < n - 1]).astype(F32)
    operands = (
        cells,
        target[0],
        win,
        w2,
        w3,
        v2,
        v3,
        wout,
        wout.T,
        jnp.broadcast_to(in_b[:, None], (c, t)),
        jnp.broadcast_to(mid_b[:, None], (c, t)),
        jnp.broadcast_to(dec_b[:, None], (c, t)),
        jnp.broadcast_to(ob, (2 * rows, t)),
        jnp.broadcast_to(edge[:, None], (2, t)),
        deint,
        inter,
    )
    res, g2, g3, gin, gout, gob, gmb, gdb = step(scale, operands, shots, rows, c, t, ka)

    gin_w = jnp.einsum("rdjri->dij", gin[:, : 4 * hr].reshape(hr, c, 2, hr, 2)).reshape(c, 4)
    gin_b = gin[:, 4 * hr].reshape(hr, c).sum(0)
    gout_w = jnp.einsum("jrird->ijd", gout.reshape(2, rl, 2, rl, c)).reshape(4, c)
    gout_b = gob.sum(1).reshape(2, rl, 2).sum(1).T.reshape(4)
    small = jnp.concatenate(
        [gin_w.reshape(-1), gin_b, gmb.sum(1), gdb.sum(1), gout_w.reshape(-1), gout_b]
    )
    flat = jnp.concatenate([g2.reshape(-1), g3.reshape(-1), small])
    per = -(-flat.shape[0] // (nd * 8 * 128)) * 8
    flat = jnp.pad(flat, (0, nd * per * 128 - flat.shape[0])).reshape(nd, per, 128)
    flat = total(flat, n).reshape(-1)

    def taps(part):
        return part.reshape(3, c, 3, c).transpose(2, 0, 1, 3)

    big = 9 * c * c
    at = [2 * big]

    def take(count):
        at[0] += count
        return flat[at[0] - count : at[0]]

    din_w = take(4 * c).reshape(c, 4)
    din_b, dmid_b, ddec_b = take(c), take(c), take(c)
    dout_w = take(4 * c).reshape(4, c)
    dout_b = take(4)
    return (
        res[None],
        din_w,
        din_b,
        taps(flat[:big]),
        dmid_b,
        taps(flat[big : 2 * big]),
        ddec_b,
        dout_w,
        dout_b,
    )


def solution(mesh):
    in_specs = (
        P("line", "gather", None, None),
        P("line", None, "gather", None),
        P(),
        P(),
        P(),
        P(),
        P(),
        P(),
        P(),
        P(),
    )
    out_specs = (P("line", None, "gather", None), P(), P(), P(), P(), P(), P(), P(), P())
    return jax.shard_map(
        per_device, mesh=mesh, in_specs=in_specs, out_specs=out_specs, check_vma=False
    )
```

```python
import functools
import math

import jax
import jax.numpy as jnp
from jax import lax
from jax.experimental import pallas as pl
from jax.experimental.pallas import tpu as pltpu
from jax.sharding import PartitionSpec as P

MESH = pl.DeviceIdType.MESH
BF = jnp.bfloat16
F32 = jnp.float32


def exchange_kernel(n, x_ref, out_ref, held, send_sem, recv_sem):
    line = lax.axis_index("line")
    me = lax.axis_index("gather")
    barrier = pltpu.get_barrier_semaphore()

    def greet(k, carry):
        peer = lax.rem(me + k, n)
        pl.semaphore_signal(barrier, inc=1, device_id=(line, peer), device_id_type=MESH)
        return carry

    lax.fori_loop(1, n, greet, 0)
    pl.semaphore_wait(barrier, n - 1)

    def copy(src, slot, peer, sem):
        return pltpu.make_async_remote_copy(
            src_ref=x_ref.at[src],
            dst_ref=held.at[slot],
            send_sem=send_sem.at[sem],
            recv_sem=recv_sem.at[slot],
            device_id=(line, peer),
            device_id_type=MESH,
        )

    def send(k, carry):
        peer = lax.rem(me + k, n)
        copy(peer, me, peer, k).start()
        return carry

    lax.fori_loop(1, n, send, 0)
    out_ref[pl.ds(me, 1)] = x_ref[pl.ds(me, 1)]

    def finish(k, carry):
        peer = lax.rem(me + k, n)
        source = lax.rem(me + n - k, n)
        copy(peer, source, peer, k).wait_recv()
        copy(peer, source, peer, k).wait_send()
        out_ref[pl.ds(source, 1)] = held[pl.ds(source, 1)]
        return carry

    lax.fori_loop(1, n, finish, 0)


def exchange(x):
    n = x.shape[0]
    return pl.pallas_call(
        functools.partial(exchange_kernel, n),
        out_shape=jax.ShapeDtypeStruct(x.shape, x.dtype),
        in_specs=[pl.BlockSpec(memory_space=pltpu.VMEM)],
        out_specs=pl.BlockSpec(memory_space=pltpu.VMEM),
        scratch_shapes=[
            pltpu.VMEM(x.shape, x.dtype),
            pltpu.SemaphoreType.DMA((n,)),
            pltpu.SemaphoreType.DMA((n,)),
        ],
        compiler_params=pltpu.CompilerParams(
            collective_id=0, has_side_effects=True, vmem_limit_bytes=16 << 20
        ),
    )(x)


def total_kernel(
    chips, n, x_ref, out_ref, half, mine, held, result, pair_sem, send_sem, recv_sem, back_sem, done_sem, on_sem, end_sem
):
    flat = lax.axis_index("line") * n + lax.axis_index("gather")
    chip = flat // 2
    core = lax.rem(flat, 2)

    def at(peer, which):
        there = 2 * peer + which
        return (there // n, lax.rem(there, n))

    barrier = pltpu.get_barrier_semaphore()
    partner = at(chip, 1 - core)
    pl.semaphore_signal(barrier, inc=1, device_id=partner, device_id_type=MESH)

    def greet(k, carry):
        peer = lax.rem(chip + k, chips)
        pl.semaphore_signal(barrier, inc=1, device_id=at(peer, core), device_id_type=MESH)
        return carry

    lax.fori_loop(1, chips, greet, 0)
    pl.semaphore_wait(barrier, chips)

    def remote(src, dst, send, recv, device):
        return pltpu.make_async_remote_copy(
            src_ref=src, dst_ref=dst, send_sem=send, recv_sem=recv, device_id=device, device_id_type=MESH
        )

    swap = remote(x_ref.at[1 - core], half, pair_sem.at[0], pair_sem.at[1], partner)
    swap.start()
    swap.wait()
    mine[...] = x_ref[core] + half[...]

    def part(src, slot, peer, sem):
        return remote(mine.at[src], held.at[slot], send_sem.at[sem], recv_sem.at[slot], at(peer, core))

    def whole(slot, peer, sem):
        where = result.at[core, slot]
        return remote(where, where, back_sem.at[sem], done_sem.at[slot], at(peer, core))

    def over(which, slot):
        where = result.at[which, slot]
        return remote(where, where, on_sem.at[slot], end_sem.at[slot], partner)

    def send(k, carry):
        peer = lax.rem(chip + k, chips)
        part(peer, chip, peer, k).start()
        return carry

    lax.fori_loop(1, chips, send, 0)

    def add(k, acc):
        source = lax.rem(chip + chips - k, chips)
        part(source, source, source, k).wait_recv()
        return acc + held[source]

    result[core, chip] = lax.fori_loop(1, chips, add, mine[chip])

    def spread(k, carry):
        peer = lax.rem(chip + k, chips)
        whole(chip, peer, k).start()
        return carry

    lax.fori_loop(1, chips, spread, 0)
    over(core, chip).start()

    def forward(k, carry):
        source = lax.rem(chip + chips - k, chips)
        whole(source, source, k).wait_recv()
        over(core, source).start()
        return carry

    lax.fori_loop(1, chips, forward, 0)

    def finish(k, carry):
        peer = lax.rem(chip + k, chips)
        part(peer, chip, peer, k).wait_send()
        whole(chip, peer, k).wait_send()
        return carry

    lax.fori_loop(1, chips, finish, 0)

    def close(k, carry):
        over(core, k).wait_send()
        over(1 - core, k).wait_recv()
        return carry

    lax.fori_loop(0, chips, close, 0)
    out_ref[...] = result[...]


def total(x, n):
    chips, per, wide = x.shape[1:]
    sems = pltpu.SemaphoreType.DMA((chips,))
    part = pltpu.VMEM((chips, per, wide), F32)
    return pl.pallas_call(
        functools.partial(total_kernel, chips, n),
        out_shape=jax.ShapeDtypeStruct(x.shape, x.dtype),
        in_specs=[pl.BlockSpec(memory_space=pltpu.VMEM)],
        out_specs=pl.BlockSpec(memory_space=pltpu.VMEM),
        scratch_shapes=[part, part, part, pltpu.VMEM(x.shape, F32), pltpu.SemaphoreType.DMA((2,))]
        + [sems] * 6,
        compiler_params=pltpu.CompilerParams(
            collective_id=1, has_side_effects=True, vmem_limit_bytes=16 << 20
        ),
    )(x)


def unpack_kernel(x_ref, in_w_ref, in_b_ref, mid_w_ref, mid_b_ref, dec_w_ref, dec_b_ref, out_w_ref, out_b_ref):
    c = in_w_ref.shape[0]
    for a in range(3):
        for b in range(3):
            for first, ref in ((0, mid_w_ref), (3, dec_w_ref)):
                tile, side = (first + a) // 2, (first + a) % 2
                row = tile * 3 * c + b * c
                ref[a, b] = x_ref[row : row + c, side * c : (side + 1) * c]
    small = x_ref[9 * c : 10 * c]
    in_w_ref[...] = small[:, 0:4]
    flipped = small.T
    in_b_ref[...] = flipped[4:5]
    mid_b_ref[...] = flipped[5:6]
    dec_b_ref[...] = flipped[6:7]
    out_w_ref[...] = flipped[8:12]
    out_b_ref[...] = flipped[12:13, 0:4]


def unpack(x, c):
    vmem = pl.BlockSpec(memory_space=pltpu.VMEM)
    sizes = ((c, 4), (1, c), (3, 3, c, c), (1, c), (3, 3, c, c), (1, c), (4, c), (1, 4))
    return pl.pallas_call(
        unpack_kernel,
        out_shape=tuple(jax.ShapeDtypeStruct(size, F32) for size in sizes),
        in_specs=[vmem],
        out_specs=(vmem,) * len(sizes),
        compiler_params=pltpu.CompilerParams(vmem_limit_bytes=16 << 20),
    )(x)


def gate(pre):
    sig = 1.0 / (1.0 + jnp.exp(-pre))
    act = pre * sig
    return act, sig + act * (1.0 - sig)


def dot(a, b):
    return jnp.dot(a, b, preferred_element_type=F32)


def dot_t(a, b):
    return lax.dot_general(a, b, (((1,), (1,)), ((), ())), preferred_element_type=F32)


def exact_dot(x, onehot):
    hi = x.astype(BF)
    rest = x - hi.astype(F32)
    mid = rest.astype(BF)
    low = (rest - mid.astype(F32)).astype(BF)
    return dot(hi, onehot) + dot(mid, onehot) + dot(low, onehot)


def step_kernel(
    scale,
    a_ref,
    target_ref,
    in_w_ref,
    in_b_ref,
    mid_w_ref,
    mid_b_ref,
    dec_w_ref,
    dec_b_ref,
    out_w_ref,
    out_b_ref,
    res_ref,
    pack_ref,
    h_ref,
    z_ref,
    e3_ref,
    e2_ref,
    e1_ref,
    h3_ref,
    s1_ref,
    s2_ref,
    s3_ref,
    win_ref,
    wide_ref,
    w2_ref,
    w3_ref,
    v2_ref,
    v3_ref,
    wout_ref,
    woutt_ref,
    ib_ref,
    mb_ref,
    db_ref,
    ob_ref,
    deint_ref,
    inter_ref,
    g2_ref,
    g3_ref,
    gin_ref,
    gout_ref,
    gob_ref,
    gmb_ref,
    gdb_ref,
):
    shots, rows = target_ref.shape[0], target_ref.shape[1]
    rl = rows // 2
    hr = rl + 2
    c = ib_ref.shape[0]
    t = ib_ref.shape[1]
    ka = a_ref.shape[1]

    def grid(height, width):
        return (
            lax.broadcasted_iota(jnp.int32, (height, width), 0),
            lax.broadcasted_iota(jnp.int32, (height, width), 1),
        )

    def onehot(mask):
        return jnp.where(mask, 1.0, 0.0).astype(BF)

    for src, fwd, back in ((mid_w_ref, w2_ref, v2_ref), (dec_w_ref, w3_ref, v3_ref)):
        for q in range(9):
            wide_ref[:, q * c : (q + 1) * c] = src[q // 3, q % 3].astype(F32)
        fwd[...] = wide_ref[...].astype(BF)
        for q in range(9):
            wide_ref[:, q * c : (q + 1) * c] = src[2 - q // 3, q % 3].astype(F32).T
        back[...] = wide_ref[...].astype(BF)
    for src, dst in ((in_b_ref, ib_ref), (mid_b_ref, mb_ref), (dec_b_ref, db_ref)):
        dst[...] = jnp.broadcast_to(src[...], (t, c)).T
    row, col = grid(4, ka)
    for r in range(hr):
        spot = onehot(col == lax.rem(row, 2) * 2 * hr + 2 * r + row // 2)
        win_ref[r * c : (r + 1) * c] = dot(in_w_ref[...], spot).astype(BF)
    row, col = grid(4, 2 * rows)
    for r in range(rl):
        spot = onehot(col == lax.rem(row, 2) * rows + 2 * r + row // 2).astype(F32)
        block = lax.dot_general(
            out_w_ref[...].astype(F32), spot, (((0,), (0,)), ((), ())), preferred_element_type=F32
        )
        woutt_ref[r * c : (r + 1) * c] = block.astype(BF)
    wout_ref[...] = woutt_ref[...].astype(F32).T.astype(BF)
    row, col = grid(2 * rows, t)
    sample = lax.rem(row, 2) * 2 + row // rows
    spread = jnp.zeros((2 * rows, t), F32)
    for k in range(4):
        spread = jnp.where(sample == k, out_b_ref[0:1, k : k + 1], spread)
    ob_ref[...] = spread
    row, col = grid(2 * t, 2 * t)
    deint_ref[...] = onehot(row == 2 * lax.rem(col, t) + col // t)
    inter_ref[...] = onehot(col == 2 * lax.rem(row, t) + row // t)
    me = lax.axis_index("gather")
    low = jnp.where(me > 0, 1.0, 0.0)
    high = jnp.where(me < shots - 1, 1.0, 0.0)

    lane = lax.broadcasted_iota(jnp.int32, (c, t), 1)
    first, last = lane == 0, lane == t - 1

    def later(x):
        return jnp.where(first, 0.0, pltpu.roll(x, 1, 1)).astype(BF)

    def sooner(x):
        return jnp.where(last, 0.0, pltpu.roll(x, t - 1, 1)).astype(BF)

    def band(ref, r):
        return ref[r : r + 3].reshape(3 * 3 * c, t)

    for r in range(rl):
        for slot in (0, shots + 1):
            z_ref[r, slot] = jnp.zeros((3 * c, t), BF)
            e3_ref[r, slot] = jnp.zeros((3 * c, t), BF)
    for slot in (0, 1, rl + 2, rl + 3):
        e2_ref[slot] = jnp.zeros((3 * c, t), BF)
    for ref in (g2_ref, g3_ref, gin_ref, gout_ref, gob_ref, gmb_ref, gdb_ref):
        ref[...] = jnp.zeros_like(ref)

    def encode(s, carry):
        pre1 = dot(win_ref[...], a_ref[s])
        for r in range(hr):
            act, slope = gate(pre1[r * c : (r + 1) * c] + ib_ref[...])
            if r == 0:
                act, slope = act * low, slope * low
            if r == hr - 1:
                act, slope = act * high, slope * high
            s1_ref[s, r] = slope
            h_ref[s, r, 0:c] = later(act)
            h_ref[s, r, c : 2 * c] = act.astype(BF)
            h_ref[s, r, 2 * c : 3 * c] = sooner(act)
        for r in range(0, rl, 2):
            wide = jnp.concatenate(
                [h_ref[s, r + q : r + q + 3].reshape(9 * c, t) for q in range(2)], axis=1
            )
            pre2 = dot(w2_ref[...], wide)
            for q in range(2):
                act, slope = gate(pre2[:, q * t : (q + 1) * t] + mb_ref[...])
                s2_ref[s, r + q] = slope
                z_ref[r + q, s + 1, 0:c] = later(act)
                z_ref[r + q, s + 1, c : 2 * c] = act.astype(BF)
                z_ref[r + q, s + 1, 2 * c : 3 * c] = sooner(act)
        return carry

    lax.fori_loop(0, shots, encode, 0)

    def decode(s, carry):
        for r in range(0, rl, 2):
            wide = jnp.concatenate(
                [z_ref[r + q, pl.ds(s, 3)].reshape(9 * c, t) for q in range(2)], axis=1
            )
            pre3 = dot(w3_ref[...], wide)
            for q in range(2):
                act, slope = gate(pre3[:, q * t : (q + 1) * t] + db_ref[...])
                s3_ref[r + q] = slope
                h3_ref[(r + q) * c : (r + q + 1) * c] = act.astype(BF)
        truth = exact_dot(target_ref[s], deint_ref[...])
        truth = jnp.concatenate([truth[:, :t], truth[:, t:]], axis=0)
        resid = dot(wout_ref[...], h3_ref[...]) + ob_ref[...] - truth
        side = jnp.concatenate([resid[:rows], resid[rows:]], axis=1)
        res_ref[s] = exact_dot(side, inter_ref[...])
        g = resid * scale
        gob_ref[...] += g
        g = g.astype(BF)
        gout_ref[...] += dot_t(h3_ref[...], g)
        back3 = dot(woutt_ref[...], g)
        bias = gdb_ref[...]
        for r in range(rl):
            e = back3[r * c : (r + 1) * c].astype(BF).astype(F32) * s3_ref[r]
            bias = bias + e
            e3_ref[r, s + 1, 0:c] = sooner(e)
            e3_ref[r, s + 1, c : 2 * c] = e.astype(BF)
            e3_ref[r, s + 1, 2 * c : 3 * c] = later(e)
        gdb_ref[...] = bias
        left = jnp.concatenate([e3_ref[r, s + 1] for r in range(rl)], axis=1)
        right = jnp.concatenate(
            [z_ref[r, pl.ds(s, 3), c : 2 * c].reshape(3 * c, t) for r in range(rl)], axis=1
        )
        g3_ref[...] += dot_t(left, right)
        return carry

    lax.fori_loop(0, shots, decode, 0)

    def pull(s, carry):
        bias = gmb_ref[...]
        for r in range(0, rl, 2):
            wide = jnp.concatenate(
                [e3_ref[r + q, pl.ds(s, 3)].reshape(9 * c, t) for q in range(2)], axis=1
            )
            back2 = dot(v3_ref[...], wide)
            for q in range(2):
                e = back2[:, q * t : (q + 1) * t].astype(BF).astype(F32) * s2_ref[s, r + q]
                bias = bias + e
                e2_ref[r + q + 2, 0:c] = sooner(e)
                e2_ref[r + q + 2, c : 2 * c] = e.astype(BF)
                e2_ref[r + q + 2, 2 * c : 3 * c] = later(e)
        gmb_ref[...] = bias
        left = jnp.concatenate([e2_ref[r + 2] for r in range(rl)], axis=1)
        right = jnp.concatenate(
            [h_ref[s, r : r + 3, c : 2 * c].reshape(3 * c, t) for r in range(rl)], axis=1
        )
        g2_ref[...] += dot_t(left, right)
        for r in range(0, hr, 2):
            wide = jnp.concatenate(
                [e2_ref[r + q : r + q + 3].reshape(9 * c, t) for q in range(2)], axis=1
            )
            back1 = dot(v2_ref[...], wide)
            for q in range(2):
                e = back1[:, q * t : (q + 1) * t].astype(BF).astype(F32) * s1_ref[s, r + q]
                e1_ref[(r + q) * c : (r + q + 1) * c] = e.astype(BF)
        gin_ref[...] += dot_t(e1_ref[...], a_ref[s])
        return carry

    lax.fori_loop(0, shots, pull, 0)

    both = jnp.concatenate([g2_ref[...], g3_ref[...]], axis=1)
    for tile in range(3):
        pack_ref[tile * 3 * c : (tile + 1) * 3 * c] = both[:, tile * t : (tile + 1) * t]
    small = jnp.zeros((c, t), F32)
    row, col = grid(ka, t)
    for r in range(hr):
        spot = onehot(
            ((row == lax.rem(col, 2) * 2 * hr + 2 * r + col // 2) & (col < 4))
            | ((row == 4 * hr) & (col == 4))
        )
        small = small + exact_dot(gin_ref[r * c : (r + 1) * c], spot)
    row, col = grid(2 * rows, t)
    k = col - 8
    for r in range(rl):
        spot = onehot(
            (k >= 0) & (k < 4) & (row == lax.rem(col, 2) * rows + 2 * r + k // 2)
        )
        small = small + exact_dot(gout_ref[r * c : (r + 1) * c], spot)
    row, col = grid(c, t)
    small = jnp.where(col == 5, jnp.sum(gmb_ref[...], axis=1, keepdims=True), small)
    small = jnp.where(col == 6, jnp.sum(gdb_ref[...], axis=1, keepdims=True), small)
    gob = jnp.sum(gob_ref[...], axis=1, keepdims=True)
    for k in range(4):
        one = jnp.sum(jnp.where(sample[:, 0:1] == k, gob, 0.0), axis=0, keepdims=True)
        small = jnp.where((col == 12) & (row == k), one, small)
    pack_ref[9 * c : 10 * c] = small
    spare = pack_ref.shape[0] - 10 * c
    if spare:
        pack_ref[10 * c :] = jnp.zeros((spare, t), F32)


def step(scale, operands, shots, rows, c, t, ka, packed):
    rl = rows // 2
    hr = rl + 2
    vmem = pl.BlockSpec(memory_space=pltpu.VMEM)
    outs = (
        jax.ShapeDtypeStruct((shots, rows, 2 * t), F32),
        jax.ShapeDtypeStruct((packed, t), F32),
    )
    scratch = [
        ((shots, hr, 3 * c, t), BF),
        ((rl, shots + 2, 3 * c, t), BF),
        ((rl, shots + 2, 3 * c, t), BF),
        ((rl + 4, 3 * c, t), BF),
        ((hr * c, t), BF),
        ((rl * c, t), BF),
        ((shots, hr, c, t), F32),
        ((shots, rl, c, t), F32),
        ((rl, c, t), F32),
        ((hr * c, ka), BF),
        ((c, 9 * c), F32),
        ((c, 9 * c), BF),
        ((c, 9 * c), BF),
        ((c, 9 * c), BF),
        ((c, 9 * c), BF),
        ((2 * rows, rl * c), BF),
        ((rl * c, 2 * rows), BF),
        ((c, t), F32),
        ((c, t), F32),
        ((c, t), F32),
        ((2 * rows, t), F32),
        ((2 * t, 2 * t), BF),
        ((2 * t, 2 * t), BF),
        ((3 * c, 3 * c), F32),
        ((3 * c, 3 * c), F32),
        ((hr * c, ka), F32),
        ((rl * c, 2 * rows), F32),
        ((2 * rows, t), F32),
        ((c, t), F32),
        ((c, t), F32),
    ]
    return pl.pallas_call(
        functools.partial(step_kernel, scale),
        out_shape=outs,
        in_specs=[vmem] * len(operands),
        out_specs=(vmem,) * len(outs),
        scratch_shapes=[pltpu.VMEM(size, kind) for size, kind in scratch],
        compiler_params=pltpu.CompilerParams(vmem_limit_bytes=56 << 20),
        cost_estimate=pl.CostEstimate(
            flops=2 * 6 * 9 * c * c * shots * rl * t,
            bytes_accessed=2 << 20,
            transcendentals=3 * c * shots * rl * t,
        ),
    )(*operands)


def per_device(noisy, target, in_w, in_b, mid_w, mid_b, dec_w, dec_b, out_w, out_b):
    lines, n = lax.axis_size("line"), lax.axis_size("gather")
    nd = lines * n
    recv, nt = noisy.shape[2], noisy.shape[3]
    shots, rows = target.shape[1], target.shape[2]
    c, t, rl = in_w.shape[0], nt // 2, rows // 2
    hr = rl + 2
    scale = 1.0 / math.sqrt(lines * n * recv * nt)
    ka = -(-(4 * hr + 1) // 16) * 16

    when = jnp.arange(nt)
    deint = (when[:, None] == (2 * (when % t) + when // t)[None, :]).astype(BF)
    wanted = (jnp.arange(n)[:, None] * rows + jnp.arange(2 * hr)[None, :] - 2).reshape(-1)
    select = (wanted[:, None] == jnp.arange(recv)[None, :]).astype(BF)
    picked = dot(select, noisy[0, 0]).astype(BF)
    picked = dot(picked, deint).astype(BF).reshape(n, 2 * hr, nt)
    tail = jnp.zeros((n, ka - 4 * hr, t), BF).at[:, 0].set(1.0)
    blocks = jnp.concatenate([picked[..., :t], picked[..., t:], tail], axis=1)
    cells = exchange(blocks)

    per = -(-10 * c // (8 * nd)) * 8
    operands = (
        cells,
        target[0],
        in_w,
        in_b[None],
        mid_w,
        mid_b[None],
        dec_w,
        dec_b[None],
        out_w,
        out_b[None],
    )
    res, pack = step(scale, operands, shots, rows, c, t, ka, nd * per)
    pack = total(pack.reshape(2, nd // 2, per, t), n).reshape(nd * per, t)
    din_w, din_b, dmid_w, dmid_b, ddec_w, ddec_b, dout_w, dout_b = unpack(pack, c)
    return (
        res[None],
        din_w,
        din_b[0],
        dmid_w,
        dmid_b[0],
        ddec_w,
        ddec_b[0],
        dout_w,
        dout_b[0],
    )


def solution(mesh):
    in_specs = (
        P("line", "gather", None, None),
        P("line", None, "gather", None),
        P(),
        P(),
        P(),
        P(),
        P(),
        P(),
        P(),
        P(),
    )
    out_specs = (P("line", None, "gather", None), P(), P(), P(), P(), P(), P(), P(), P())
    return jax.shard_map(
        per_device, mesh=mesh, in_specs=in_specs, out_specs=out_specs, check_vma=False
    )
```

```python
import functools
import math

import jax
import jax.numpy as jnp
from jax import lax
from jax.experimental import pallas as pl
from jax.experimental.pallas import tpu as pltpu
from jax.sharding import PartitionSpec as P

MESH = pl.DeviceIdType.MESH
BF = jnp.bfloat16
F32 = jnp.float32


def exchange_kernel(n, x_ref, out_ref, held, send_sem, recv_sem):
    line = lax.axis_index("line")
    me = lax.axis_index("gather")
    barrier = pltpu.get_barrier_semaphore()

    def greet(k, carry):
        peer = lax.rem(me + k, n)
        pl.semaphore_signal(barrier, inc=1, device_id=(line, peer), device_id_type=MESH)
        return carry

    lax.fori_loop(1, n, greet, 0)
    pl.semaphore_wait(barrier, n - 1)

    def copy(src, slot, peer, sem):
        return pltpu.make_async_remote_copy(
            src_ref=x_ref.at[src],
            dst_ref=held.at[slot],
            send_sem=send_sem.at[sem],
            recv_sem=recv_sem.at[slot],
            device_id=(line, peer),
            device_id_type=MESH,
        )

    def send(k, carry):
        peer = lax.rem(me + k, n)
        copy(peer, me, peer, k).start()
        return carry

    lax.fori_loop(1, n, send, 0)
    out_ref[pl.ds(me, 1)] = x_ref[pl.ds(me, 1)]

    def finish(k, carry):
        peer = lax.rem(me + k, n)
        source = lax.rem(me + n - k, n)
        copy(peer, source, peer, k).wait_recv()
        copy(peer, source, peer, k).wait_send()
        out_ref[pl.ds(source, 1)] = held[pl.ds(source, 1)]
        return carry

    lax.fori_loop(1, n, finish, 0)


def exchange(x):
    n = x.shape[0]
    return pl.pallas_call(
        functools.partial(exchange_kernel, n),
        out_shape=jax.ShapeDtypeStruct(x.shape, x.dtype),
        in_specs=[pl.BlockSpec(memory_space=pltpu.VMEM)],
        out_specs=pl.BlockSpec(memory_space=pltpu.VMEM),
        scratch_shapes=[
            pltpu.VMEM(x.shape, x.dtype),
            pltpu.SemaphoreType.DMA((n,)),
            pltpu.SemaphoreType.DMA((n,)),
        ],
        compiler_params=pltpu.CompilerParams(
            collective_id=0, has_side_effects=True, vmem_limit_bytes=16 << 20
        ),
    )(x)


def total_kernel(
    chips, n, x_ref, out_ref, half, mine, held, result, pair_sem, send_sem, recv_sem, back_sem, done_sem, on_sem, end_sem
):
    flat = lax.axis_index("line") * n + lax.axis_index("gather")
    chip = flat // 2
    core = lax.rem(flat, 2)

    def at(peer, which):
        there = 2 * peer + which
        return (there // n, lax.rem(there, n))

    barrier = pltpu.get_barrier_semaphore()
    partner = at(chip, 1 - core)
    pl.semaphore_signal(barrier, inc=1, device_id=partner, device_id_type=MESH)

    def greet(k, carry):
        peer = lax.rem(chip + k, chips)
        pl.semaphore_signal(barrier, inc=1, device_id=at(peer, core), device_id_type=MESH)
        return carry

    lax.fori_loop(1, chips, greet, 0)
    pl.semaphore_wait(barrier, chips)

    def remote(src, dst, send, recv, device):
        return pltpu.make_async_remote_copy(
            src_ref=src, dst_ref=dst, send_sem=send, recv_sem=recv, device_id=device, device_id_type=MESH
        )

    swap = remote(x_ref.at[1 - core], half, pair_sem.at[0], pair_sem.at[1], partner)
    swap.start()
    swap.wait()
    mine[...] = x_ref[core] + half[...]

    def part(src, slot, peer, sem):
        return remote(mine.at[src], held.at[slot], send_sem.at[sem], recv_sem.at[slot], at(peer, core))

    def whole(slot, peer, sem):
        where = result.at[core, slot]
        return remote(where, where, back_sem.at[sem], done_sem.at[slot], at(peer, core))

    def over(which, slot):
        where = result.at[which, slot]
        return remote(where, where, on_sem.at[slot], end_sem.at[slot], partner)

    def send(k, carry):
        peer = lax.rem(chip + k, chips)
        part(peer, chip, peer, k).start()
        return carry

    lax.fori_loop(1, chips, send, 0)

    def add(k, acc):
        source = lax.rem(chip + chips - k, chips)
        part(source, source, source, k).wait_recv()
        return acc + held[source]

    result[core, chip] = lax.fori_loop(1, chips, add, mine[chip])

    def spread(k, carry):
        peer = lax.rem(chip + k, chips)
        whole(chip, peer, k).start()
        return carry

    lax.fori_loop(1, chips, spread, 0)
    over(core, chip).start()

    def forward(k, carry):
        source = lax.rem(chip + chips - k, chips)
        whole(source, source, k).wait_recv()
        over(core, source).start()
        return carry

    lax.fori_loop(1, chips, forward, 0)

    def finish(k, carry):
        peer = lax.rem(chip + k, chips)
        part(peer, chip, peer, k).wait_send()
        whole(chip, peer, k).wait_send()
        return carry

    lax.fori_loop(1, chips, finish, 0)

    def close(k, carry):
        over(core, k).wait_send()
        over(1 - core, k).wait_recv()
        return carry

    lax.fori_loop(0, chips, close, 0)
    out_ref[...] = result[...]


def total(x, n):
    chips, per, wide = x.shape[1:]
    sems = pltpu.SemaphoreType.DMA((chips,))
    part = pltpu.VMEM((chips, per, wide), F32)
    return pl.pallas_call(
        functools.partial(total_kernel, chips, n),
        out_shape=jax.ShapeDtypeStruct(x.shape, x.dtype),
        in_specs=[pl.BlockSpec(memory_space=pltpu.VMEM)],
        out_specs=pl.BlockSpec(memory_space=pltpu.VMEM),
        scratch_shapes=[part, part, part, pltpu.VMEM(x.shape, F32), pltpu.SemaphoreType.DMA((2,))]
        + [sems] * 6,
        compiler_params=pltpu.CompilerParams(
            collective_id=1, has_side_effects=True, vmem_limit_bytes=16 << 20
        ),
    )(x)


def unpack_kernel(x_ref, in_w_ref, in_b_ref, mid_w_ref, mid_b_ref, dec_w_ref, dec_b_ref, out_w_ref, out_b_ref):
    c = in_w_ref.shape[0]
    for a in range(3):
        for b in range(3):
            for first, ref in ((0, mid_w_ref), (3, dec_w_ref)):
                tile, side = (first + a) // 2, (first + a) % 2
                row = tile * 3 * c + b * c
                ref[a, b] = x_ref[row : row + c, side * c : (side + 1) * c]
    small = x_ref[9 * c : 10 * c]
    in_w_ref[...] = small[:, 0:4]
    flipped = small.T
    in_b_ref[...] = flipped[4:5]
    mid_b_ref[...] = flipped[5:6]
    dec_b_ref[...] = flipped[6:7]
    out_w_ref[...] = flipped[8:12]
    out_b_ref[...] = flipped[12:13, 0:4]


def unpack(x, c):
    vmem = pl.BlockSpec(memory_space=pltpu.VMEM)
    sizes = ((c, 4), (1, c), (3, 3, c, c), (1, c), (3, 3, c, c), (1, c), (4, c), (1, 4))
    return pl.pallas_call(
        unpack_kernel,
        out_shape=tuple(jax.ShapeDtypeStruct(size, F32) for size in sizes),
        in_specs=[vmem],
        out_specs=(vmem,) * len(sizes),
        compiler_params=pltpu.CompilerParams(vmem_limit_bytes=16 << 20),
    )(x)


def gate(pre):
    sig = 0.5 * jnp.tanh(0.5 * pre) + 0.5
    act = pre * sig
    return act, sig + act * (1.0 - sig)


def dot(a, b):
    return jnp.dot(a, b, preferred_element_type=F32)


def dot_t(a, b):
    return lax.dot_general(a, b, (((1,), (1,)), ((), ())), preferred_element_type=F32)


def exact_dot(x, onehot):
    hi = x.astype(BF)
    rest = x - hi.astype(F32)
    mid = rest.astype(BF)
    low = (rest - mid.astype(F32)).astype(BF)
    size = x.shape[0]
    pieces = jnp.concatenate([hi.astype(F32), mid.astype(F32), low.astype(F32)], axis=0).astype(BF)
    out = dot(pieces, onehot)
    return out[:size] + out[size : 2 * size] + out[2 * size :]


def step_kernel(
    scale,
    a_ref,
    target_ref,
    in_w_ref,
    in_b_ref,
    mid_w_ref,
    mid_b_ref,
    dec_w_ref,
    dec_b_ref,
    out_w_ref,
    out_b_ref,
    res_ref,
    pack_ref,
    h_ref,
    z_ref,
    e3_ref,
    e2_ref,
    e1_ref,
    h3_ref,
    s1_ref,
    s2_ref,
    s3_ref,
    win_ref,
    wide_ref,
    w2_ref,
    w3_ref,
    v2_ref,
    v3_ref,
    wout_ref,
    woutt_ref,
    ib_ref,
    mb_ref,
    db_ref,
    ob_ref,
    deint_ref,
    inter_ref,
    g2_ref,
    g3_ref,
    gin_ref,
    gout_ref,
    gob_ref,
    gmb_ref,
    gdb_ref,
):
    shots, rows = target_ref.shape[0], target_ref.shape[1]
    rl = rows // 2
    hr = rl + 2
    c = ib_ref.shape[0]
    t = ib_ref.shape[1]
    ka = a_ref.shape[1]

    def grid(height, width):
        return (
            lax.broadcasted_iota(jnp.int32, (height, width), 0),
            lax.broadcasted_iota(jnp.int32, (height, width), 1),
        )

    def onehot(mask):
        return jnp.where(mask, 1.0, 0.0).astype(BF)

    for src, fwd, back in ((mid_w_ref, w2_ref, v2_ref), (dec_w_ref, w3_ref, v3_ref)):
        for q in range(9):
            wide_ref[:, q * c : (q + 1) * c] = src[q // 3, q % 3].astype(F32)
        fwd[...] = wide_ref[...].astype(BF)
        for q in range(9):
            wide_ref[:, q * c : (q + 1) * c] = src[2 - q // 3, q % 3].astype(F32).T
        back[...] = wide_ref[...].astype(BF)
    for src, dst in ((in_b_ref, ib_ref), (mid_b_ref, mb_ref), (dec_b_ref, db_ref)):
        dst[...] = jnp.broadcast_to(src[...], (t, c)).T
    row, col = grid(4, ka)
    for r in range(hr):
        spot = onehot(col == lax.rem(row, 2) * 2 * hr + 2 * r + row // 2)
        win_ref[r * c : (r + 1) * c] = dot(in_w_ref[...], spot).astype(BF)
    row, col = grid(4, 2 * rows)
    for r in range(rl):
        spot = onehot(col == lax.rem(row, 2) * rows + 2 * r + row // 2).astype(F32)
        block = lax.dot_general(
            out_w_ref[...].astype(F32), spot, (((0,), (0,)), ((), ())), preferred_element_type=F32
        )
        woutt_ref[r * c : (r + 1) * c] = block.astype(BF)
    wout_ref[...] = woutt_ref[...].astype(F32).T.astype(BF)
    row, col = grid(2 * rows, t)
    sample = lax.rem(row, 2) * 2 + row // rows
    spread = jnp.zeros((2 * rows, t), F32)
    for k in range(4):
        spread = jnp.where(sample == k, out_b_ref[0:1, k : k + 1], spread)
    ob_ref[...] = spread
    row, col = grid(2 * t, 2 * t)
    deint_ref[...] = onehot(row == 2 * lax.rem(col, t) + col // t)
    inter_ref[...] = onehot(col == 2 * lax.rem(row, t) + row // t)
    me = lax.axis_index("gather")
    low = jnp.where(me > 0, 1.0, 0.0)
    high = jnp.where(me < shots - 1, 1.0, 0.0)

    lane = lax.broadcasted_iota(jnp.int32, (c, t), 1)
    first, last = lane == 0, lane == t - 1

    def later(x):
        return jnp.where(first, jnp.zeros((), BF), pltpu.roll(x.astype(BF), 1, 1))

    def sooner(x):
        return jnp.where(last, jnp.zeros((), BF), pltpu.roll(x.astype(BF), t - 1, 1))

    def band(ref, r):
        return ref[r : r + 3].reshape(3 * 3 * c, t)

    for r in range(rl):
        for slot in (0, shots + 1):
            z_ref[r, slot] = jnp.zeros((3 * c, t), BF)
            e3_ref[r, slot] = jnp.zeros((3 * c, t), BF)
    for slot in (0, 1, rl + 2, rl + 3):
        e2_ref[slot] = jnp.zeros((3 * c, t), BF)
    for ref in (g2_ref, g3_ref, gin_ref, gout_ref, gob_ref, gmb_ref, gdb_ref):
        ref[...] = jnp.zeros_like(ref)

    def encode(s, carry):
        pre1 = dot(win_ref[...], a_ref[s])
        for r in range(hr):
            act, slope = gate(pre1[r * c : (r + 1) * c] + ib_ref[...])
            if r == 0:
                act, slope = act * low, slope * low
            if r == hr - 1:
                act, slope = act * high, slope * high
            s1_ref[s, r] = slope
            h_ref[s, r, 0:c] = later(act)
            h_ref[s, r, c : 2 * c] = act.astype(BF)
            h_ref[s, r, 2 * c : 3 * c] = sooner(act)
        for r in range(0, rl, 2):
            wide = jnp.concatenate(
                [h_ref[s, r + q : r + q + 3].reshape(9 * c, t) for q in range(2)], axis=1
            )
            pre2 = dot(w2_ref[...], wide)
            for q in range(2):
                act, slope = gate(pre2[:, q * t : (q + 1) * t] + mb_ref[...])
                s2_ref[s, r + q] = slope
                z_ref[r + q, s + 1, 0:c] = later(act)
                z_ref[r + q, s + 1, c : 2 * c] = act.astype(BF)
                z_ref[r + q, s + 1, 2 * c : 3 * c] = sooner(act)
        return carry

    lax.fori_loop(0, shots, encode, 0, unroll=8)

    def decode(s, carry):
        for r in range(0, rl, 2):
            wide = jnp.concatenate(
                [z_ref[r + q, pl.ds(s, 3)].reshape(9 * c, t) for q in range(2)], axis=1
            )
            pre3 = dot(w3_ref[...], wide)
            for q in range(2):
                act, slope = gate(pre3[:, q * t : (q + 1) * t] + db_ref[...])
                s3_ref[r + q] = slope
                h3_ref[(r + q) * c : (r + q + 1) * c] = act.astype(BF)
        truth = exact_dot(target_ref[s], deint_ref[...])
        truth = jnp.concatenate([truth[:, :t], truth[:, t:]], axis=0)
        resid = dot(wout_ref[...], h3_ref[...]) + ob_ref[...] - truth
        side = jnp.concatenate([resid[:rows], resid[rows:]], axis=1)
        res_ref[s] = exact_dot(side, inter_ref[...])
        g = resid * scale
        gob_ref[...] += g
        g = g.astype(BF)
        gout_ref[...] += dot_t(h3_ref[...], g)
        back3 = dot(woutt_ref[...], g)
        bias = gdb_ref[...]
        for r in range(rl):
            e = back3[r * c : (r + 1) * c].astype(BF).astype(F32) * s3_ref[r]
            bias = bias + e
            e3_ref[r, s + 1, 0:c] = sooner(e)
            e3_ref[r, s + 1, c : 2 * c] = e.astype(BF)
            e3_ref[r, s + 1, 2 * c : 3 * c] = later(e)
        gdb_ref[...] = bias
        left = jnp.concatenate([e3_ref[r, s + 1] for r in range(rl)], axis=1)
        right = jnp.concatenate(
            [z_ref[r, pl.ds(s, 3), c : 2 * c].reshape(3 * c, t) for r in range(rl)], axis=1
        )
        g3_ref[...] += dot_t(left, right)
        return carry

    lax.fori_loop(0, shots, decode, 0, unroll=8)

    def pull(s, carry):
        bias = gmb_ref[...]
        for r in range(0, rl, 2):
            wide = jnp.concatenate(
                [e3_ref[r + q, pl.ds(s, 3)].reshape(9 * c, t) for q in range(2)], axis=1
            )
            back2 = dot(v3_ref[...], wide)
            for q in range(2):
                e = back2[:, q * t : (q + 1) * t].astype(BF).astype(F32) * s2_ref[s, r + q]
                bias = bias + e
                e2_ref[r + q + 2, 0:c] = sooner(e)
                e2_ref[r + q + 2, c : 2 * c] = e.astype(BF)
                e2_ref[r + q + 2, 2 * c : 3 * c] = later(e)
        gmb_ref[...] = bias
        left = jnp.concatenate([e2_ref[r + 2] for r in range(rl)], axis=1)
        right = jnp.concatenate(
            [h_ref[s, r : r + 3, c : 2 * c].reshape(3 * c, t) for r in range(rl)], axis=1
        )
        g2_ref[...] += dot_t(left, right)
        for r in range(0, hr, 2):
            wide = jnp.concatenate(
                [e2_ref[r + q : r + q + 3].reshape(9 * c, t) for q in range(2)], axis=1
            )
            back1 = dot(v2_ref[...], wide)
            for q in range(2):
                e = back1[:, q * t : (q + 1) * t].astype(BF).astype(F32) * s1_ref[s, r + q]
                e1_ref[(r + q) * c : (r + q + 1) * c] = e.astype(BF)
        gin_ref[...] += dot_t(e1_ref[...], a_ref[s])
        return carry

    lax.fori_loop(0, shots, pull, 0, unroll=8)

    both = jnp.concatenate([g2_ref[...], g3_ref[...]], axis=1)
    for tile in range(3):
        pack_ref[tile * 3 * c : (tile + 1) * 3 * c] = both[:, tile * t : (tile + 1) * t]
    small = jnp.zeros((c, t), F32)
    row, col = grid(ka, t)
    for r in range(hr):
        spot = onehot(
            ((row == lax.rem(col, 2) * 2 * hr + 2 * r + col // 2) & (col < 4))
            | ((row == 4 * hr) & (col == 4))
        )
        small = small + exact_dot(gin_ref[r * c : (r + 1) * c], spot)
    row, col = grid(2 * rows, t)
    k = col - 8
    for r in range(rl):
        spot = onehot(
            (k >= 0) & (k < 4) & (row == lax.rem(col, 2) * rows + 2 * r + k // 2)
        )
        small = small + exact_dot(gout_ref[r * c : (r + 1) * c], spot)
    row, col = grid(c, t)
    small = jnp.where(col == 5, jnp.sum(gmb_ref[...], axis=1, keepdims=True), small)
    small = jnp.where(col == 6, jnp.sum(gdb_ref[...], axis=1, keepdims=True), small)
    gob = jnp.sum(gob_ref[...], axis=1, keepdims=True)
    for k in range(4):
        one = jnp.sum(jnp.where(sample[:, 0:1] == k, gob, 0.0), axis=0, keepdims=True)
        small = jnp.where((col == 12) & (row == k), one, small)
    pack_ref[9 * c : 10 * c] = small
    spare = pack_ref.shape[0] - 10 * c
    if spare:
        pack_ref[10 * c :] = jnp.zeros((spare, t), F32)


def step(scale, operands, shots, rows, c, t, ka, packed):
    rl = rows // 2
    hr = rl + 2
    vmem = pl.BlockSpec(memory_space=pltpu.VMEM)
    outs = (
        jax.ShapeDtypeStruct((shots, rows, 2 * t), F32),
        jax.ShapeDtypeStruct((packed, t), F32),
    )
    scratch = [
        ((shots, hr, 3 * c, t), BF),
        ((rl, shots + 2, 3 * c, t), BF),
        ((rl, shots + 2, 3 * c, t), BF),
        ((rl + 4, 3 * c, t), BF),
        ((hr * c, t), BF),
        ((rl * c, t), BF),
        ((shots, hr, c, t), F32),
        ((shots, rl, c, t), F32),
        ((rl, c, t), F32),
        ((hr * c, ka), BF),
        ((c, 9 * c), F32),
        ((c, 9 * c), BF),
        ((c, 9 * c), BF),
        ((c, 9 * c), BF),
        ((c, 9 * c), BF),
        ((2 * rows, rl * c), BF),
        ((rl * c, 2 * rows), BF),
        ((c, t), F32),
        ((c, t), F32),
        ((c, t), F32),
        ((2 * rows, t), F32),
        ((2 * t, 2 * t), BF),
        ((2 * t, 2 * t), BF),
        ((3 * c, 3 * c), F32),
        ((3 * c, 3 * c), F32),
        ((hr * c, ka), F32),
        ((rl * c, 2 * rows), F32),
        ((2 * rows, t), F32),
        ((c, t), F32),
        ((c, t), F32),
    ]
    return pl.pallas_call(
        functools.partial(step_kernel, scale),
        out_shape=outs,
        in_specs=[vmem] * len(operands),
        out_specs=(vmem,) * len(outs),
        scratch_shapes=[pltpu.VMEM(size, kind) for size, kind in scratch],
        compiler_params=pltpu.CompilerParams(vmem_limit_bytes=56 << 20),
        cost_estimate=pl.CostEstimate(
            flops=2 * 6 * 9 * c * c * shots * rl * t,
            bytes_accessed=2 << 20,
            transcendentals=3 * c * shots * rl * t,
        ),
    )(*operands)


def per_device(noisy, target, in_w, in_b, mid_w, mid_b, dec_w, dec_b, out_w, out_b):
    lines, n = lax.axis_size("line"), lax.axis_size("gather")
    nd = lines * n
    recv, nt = noisy.shape[2], noisy.shape[3]
    shots, rows = target.shape[1], target.shape[2]
    c, t, rl = in_w.shape[0], nt // 2, rows // 2
    hr = rl + 2
    scale = 1.0 / math.sqrt(lines * n * recv * nt)
    ka = -(-(4 * hr + 1) // 16) * 16

    when = jnp.arange(nt)
    deint = (when[:, None] == (2 * (when % t) + when // t)[None, :]).astype(BF)
    wanted = (jnp.arange(n)[:, None] * rows + jnp.arange(2 * hr)[None, :] - 2).reshape(-1)
    select = (wanted[:, None] == jnp.arange(recv)[None, :]).astype(BF)
    picked = dot(select, noisy[0, 0]).astype(BF)
    picked = dot(picked, deint).astype(BF).reshape(n, 2 * hr, nt)
    tail = jnp.zeros((n, ka - 4 * hr, t), BF).at[:, 0].set(1.0)
    blocks = jnp.concatenate([picked[..., :t], picked[..., t:], tail], axis=1)
    cells = exchange(blocks)

    per = -(-10 * c // (8 * nd)) * 8
    operands = (
        cells,
        target[0],
        in_w,
        in_b[None],
        mid_w,
        mid_b[None],
        dec_w,
        dec_b[None],
        out_w,
        out_b[None],
    )
    res, pack = step(scale, operands, shots, rows, c, t, ka, nd * per)
    pack = total(pack.reshape(2, nd // 2, per, t), n).reshape(nd * per, t)
    din_w, din_b, dmid_w, dmid_b, ddec_w, ddec_b, dout_w, dout_b = unpack(pack, c)
    return (
        res[None],
        din_w,
        din_b[0],
        dmid_w,
        dmid_b[0],
        ddec_w,
        ddec_b[0],
        dout_w,
        dout_b[0],
    )


def solution(mesh):
    in_specs = (
        P("line", "gather", None, None),
        P("line", None, "gather", None),
        P(),
        P(),
        P(),
        P(),
        P(),
        P(),
        P(),
        P(),
    )
    out_specs = (P("line", None, "gather", None), P(), P(), P(), P(), P(), P(), P(), P())
    return jax.shard_map(
        per_device, mesh=mesh, in_specs=in_specs, out_specs=out_specs, check_vma=False
    )
```
